768 devices in a mesh: dp: 8 (over y_hi, core), mp: 96 (over y_lo, z, x).
Axes of the slice: x: 4, y: 8 (y_hi: 4, y_lo: 2; y = y_hi * 2 + y_lo), z: 12, core: 2. Of those that a mesh axis runs over, the one named last changes fastest.
Arguments:
- inputs: bfloat16 [1024, 6144], P('dp', 'mp'), may hold values from -6 to 6
- out_grad: bfloat16 [1024, 6144], P('dp', 'mp'), may hold values from -6 to 6
- first_weight: bfloat16 [6144, 12288], P('dp', 'mp'), may hold values from -0.25 to 0.25
- second_weight: bfloat16 [12288, 6144], P('mp', 'dp'), may hold values from -0.078125 to 0.078125
Outputs:
- input_grad: bfloat16 [1024, 6144], P('dp', 'mp')
- weight_grad: bfloat16 [6144, 12288], P('dp', 'mp')
The draws below stay inside these ranges and needn't reach their ends.
All inputs are finite; a program needn't handle non-finite values.
Results may differ from the reference program's by a relative error of at most 0.017.
Values may be sent and summed in bfloat16 or wider, within the bound.
A program may use at most 32 MiB of HBM per device.

```python
import math
import jax
import jax.numpy as jnp
from jax import lax

D = 6144
FF = 12288
TOK_DEV = 128
TOKENS = 1024
N_DP = 8


def with_spikes(array, stream_key, source, target, blocks, factor):
    def block_of(dim):
        return (jnp.arange(array.shape[dim]) // (array.shape[dim] // blocks)).reshape((-1,) + (1,) * (array.ndim - 1 - dim))

    first = jax.random.permutation(stream_key, blocks)[block_of(target)]
    other_side = (block_of(target) + blocks // 2) % blocks
    return jnp.where((block_of(source) == first) | (block_of(source) == other_side), factor * array, array)


def block_scale(key, shape, pieces, low, largest):
    def one(axis_at, parts):
        steps = jax.random.uniform(jax.random.fold_in(jax.random.fold_in(key, 6), axis_at), (parts,), jnp.float32, low / len(pieces), largest / len(pieces))
        return jnp.repeat(jnp.exp(steps), shape[axis_at] // parts).reshape((-1,) + (1,) * (len(shape) - axis_at - 1))

    level = one(*pieces[0])
    for cut in pieces[1:]:
        level = level * one(*cut)
    return level


def centred(rng, extent, scale, limit, pieces=(), kind=jnp.bfloat16):
    result = scale * jax.random.normal(rng, extent, jnp.float32)
    if pieces:
        result = result * block_scale(rng, extent, pieces, -0.22, 0.18)
    return jnp.clip(result, -limit, limit).astype(kind)


def bell_draw_with(stream_key, extent, width, reach, pieces, heavy, dtype=jnp.bfloat16):
    drawn = width * jax.random.normal(stream_key, extent, jnp.float32)
    if pieces:
        drawn = drawn * block_scale(stream_key, extent, pieces, -0.22, 0.18)
    return jnp.clip(with_spikes(drawn, jax.random.fold_in(stream_key, 3), *heavy), -reach, reach).astype(dtype)


def setup_inputs(seed: int = 0) -> dict:
    key_list = jax.random.split(jax.random.key(seed), 5)
    return {
        "inputs": centred(key_list[0], (TOKENS, D), 1.0, 6.0, ((0, 8), (1, 96))),
        "out_grad": centred(key_list[1], (TOKENS, D), 1.0, 6.0, ((0, 8), (1, 96))),
        "first_weight": bell_draw_with(key_list[2], (D, FF), D ** -0.5, 0.25, ((0, 8), (1, 96)), (1, 0, 96, 4.75)),
        "second_weight": centred(key_list[3], (FF, D), D ** -0.5, 0.078125, ((0, 96), (1, 8))),
    }


def activation(values):
    return jax.nn.gelu(values, approximate=False)

def reference(inputs, out_grad, first_weight, second_weight):
    hidden = jnp.dot(inputs, first_weight, preferred_element_type=jnp.float32)
    back = jnp.dot(out_grad, second_weight.T, preferred_element_type=jnp.float32)
    _, pull = jax.vjp(activation, hidden)
    act_grad = pull(back)[0].astype(jnp.bfloat16)
    input_grad = jnp.dot(act_grad, first_weight.T, preferred_element_type=jnp.float32).astype(jnp.bfloat16)
    scale = 1.0 / math.sqrt(TOKENS)
    group_inputs = inputs.reshape(N_DP, TOK_DEV, D)
    group_grads = act_grad.reshape(N_DP, TOK_DEV, FF)

    def add_group(total, pair):
        term = jnp.dot(pair[0].T, pair[1], preferred_element_type=jnp.float32) * scale
        rounded = lax.optimization_barrier(term.astype(jnp.bfloat16))
        return (total + rounded.astype(jnp.float32), None)
    summed, _ = lax.scan(add_group, jnp.zeros((D, FF), jnp.float32), (group_inputs, group_grads))
    return (input_grad, summed.astype(jnp.bfloat16))
```

```python
import functools
import math

import jax
import jax.numpy as jnp
from jax import lax
from jax.experimental import pallas as pl
from jax.experimental.pallas import tpu as pltpu
from jax.sharding import PartitionSpec as P

NX, NY, NC = 4, 8, 2
F32, BF16 = jnp.float32, jnp.bfloat16
ROOT_HALF, ROOT_TWO_PI = math.sqrt(0.5), math.sqrt(2.0 * math.pi)


def gelu_slope(v):
    cdf = 0.5 * (1.0 + lax.erf(v * ROOT_HALF))
    return cdf + v * jnp.exp(-0.5 * v * v) / ROOT_TWO_PI


def dot(a, b, ca, cb):
    return lax.dot_general(a, b, (((ca,), (cb,)), ((), ())), preferred_element_type=F32)


def kernel(nz, scale, xt, gt, w1, w2, ig_out, wg_out,
           buf, w1b, w2b, cs, cr, keep, ys, yr, actf, part, xin, far, zs, zr, fin, igr, wgs, wgr,
           loc, w_s, w_r, p1_s, p1_r, z_s, z_r, x_s, x_r, c_s, c_r, y_s, y_r, a_s, a_r, ac_s, ac_r,
           gx_s, gx_r, zz_s, zz_r, p2_s, p2_r, wg_s, wg_r):
    nj = nz // 2
    feat = xt.shape[0]
    depth = nj * feat
    tok = xt.shape[1]
    col = nz * NX
    dp, mp = lax.axis_index("dp"), lax.axis_index("mp")
    core, ylo = dp % 2, mp // col
    z, x = (mp % col) // NX, mp % NX
    y = (dp // 2) * 2 + ylo

    def at(x_, y_, z_, c_):
        return ((y_ // 2) * 2 + c_, (y_ % 2) * col + z_ * NX + x_)

    def send(src, dst, ssem, rsem, dev):
        return pltpu.make_async_remote_copy(
            src_ref=src, dst_ref=dst, send_sem=ssem, recv_sem=rsem,
            device_id=dev, device_id_type=pl.DeviceIdType.MESH)

    right, left = at((x + 1) % NX, y, z, core), at((x + 3) % NX, y, z, core)
    other = at(x, y, z, 1 - core)
    twin = at(x, y + 1 - 2 * ylo, z, core)
    ydev = [None] + [at(x, (y + d) % NY, z, core) for d in range(1, NY)]
    zdev = [None] + [at(x, y, (z + d) % nz, core) for d in range(1, nz)]
    plane, mine = mp // nj, mp % nj
    goal_z = (dp // NX) * nj + mine
    goal = (plane // 2, (plane % 2) * col + goal_z * NX + dp % NX)
    origin = ((z // nj) * NX + x, (dp * 2 + ylo) * nj + z % nj)
    stays = jnp.logical_and(goal[0] == dp, goal[1] == mp)

    half_rows = pl.ds(pl.multiple_of(ylo * depth, 128), depth)
    other_rows = pl.ds(pl.multiple_of((1 - ylo) * depth, 128), depth)
    lw1 = pltpu.make_async_copy(w1.at[half_rows, :], w1b.at[ylo], loc.at[0])
    lw2 = pltpu.make_async_copy(w2.at[:, half_rows], w2b.at[ylo], loc.at[1])
    lw1.start()
    lw2.start()

    barrier = pltpu.get_barrier_semaphore()

    def greet(dev):
        pl.semaphore_signal(barrier, inc=1, device_id=dev, device_id_type=pl.DeviceIdType.MESH)

    @pl.when(jnp.logical_not(stays))
    def _():
        greet(origin)
        greet(goal)
    for dev in [right, left, other] + ydev[1:] + zdev[1:]:
        greet(dev)
    peers = 3 + (NY - 1) + (nz - 1)

    @pl.when(stays)
    def _():
        pl.semaphore_wait(barrier, peers)

    @pl.when(jnp.logical_not(stays))
    def _():
        pl.semaphore_wait(barrier, peers + 2)

    pair = [(xt, 0), (gt, 1)]

    @pl.when(stays)
    def _():
        cps = [pltpu.make_async_copy(src, buf.at[0, goal_z, i], p1_r.at[i]) for src, i in pair]
        for cp in cps:
            cp.start()
        for cp in cps:
            cp.wait()

    @pl.when(jnp.logical_not(stays))
    def _():
        cps = [send(src, buf.at[0, goal_z, i], p1_s.at[i], p1_r.at[i], goal) for src, i in pair]
        for cp in cps:
            cp.start()
        for cp in cps:
            cp.wait()

    zcp = []
    for d in range(1, nz):
        cp = send(buf.at[0, z], buf.at[0, z], z_s.at[d - 1], z_r.at[z], zdev[d])
        cp.start()
        zcp.append(cp)
    wcp = [send(w1.at[other_rows, :], w1b.at[ylo], w_s.at[0], w_r.at[0], twin),
           send(w2.at[:, other_rows], w2b.at[ylo], w_s.at[1], w_r.at[1], twin)]
    for cp in wcp:
        cp.start()
    lw1.wait()
    lw2.wait()

    parts = [pl.ds(0, nj), pl.ds(nj, nj)]

    def xcp(way, i, rel, half):
        to = (rel + (3 if way == 0 else 1)) % NX
        return send(buf.at[rel, parts[half]], buf.at[to, parts[half]], x_s.at[way, i], x_r.at[way, i],
                    right if way == 0 else left)

    ways = [[xcp(0, 0, 0, 0), xcp(0, 1, 0, 1), xcp(0, 2, 3, 0)],
            [xcp(1, 1, 0, 0), xcp(1, 0, 0, 1), xcp(1, 2, 1, 1)]]
    for half in range(2):
        for t in range(half * nj, half * nj + nj):
            @pl.when(t != z)
            def _(t=t):
                send(buf.at[0, t], buf.at[0, t], z_s.at[0], z_r.at[t], right).wait_recv()
        ways[0][half].start()
        ways[1][half].start()
    for cp in wcp:
        cp.wait()

    def tokens(rel, which):
        pieces = [buf[rel, i * nj:(i + 1) * nj, which].reshape(depth, tok) for i in range(2)]
        return jnp.concatenate(pieces, axis=1)

    ccp = [send(cs.at[r], cr.at[r], c_s.at[r], c_r.at[r], other) for r in range(NX)]

    def project(r):
        xs, gs = tokens(r, 0), tokens(r, 1)
        cs[r, 0] = dot(w1b[1 - core], xs, 0, 0)
        cs[r, 1] = dot(w2b[1 - core], gs, 1, 0)
        ccp[r].start()
        keep[r, 0] = dot(w1b[core], xs, 0, 0)
        keep[r, 1] = dot(w2b[core], gs, 1, 0)

    ycp = {}
    rows = ys.shape[3]

    def spread(r):
        ccp[r].wait()
        for a in range(2):
            total = (keep[r, a] + cr[r, a]).astype(BF16)
            ys[r, :, a] = total.reshape(NY, rows, 2 * tok)
        for d in range(1, NY):
            cp = send(ys.at[r, (y + d) % NY], yr.at[r, d], y_s.at[r, d - 1], y_r.at[r, d - 1], ydev[d])
            cp.start()
            ycp[r, d] = cp

    project(0)
    ways[0][0].wait_recv()
    ways[0][2].start()
    ways[1][1].wait_recv()
    ways[1][2].start()
    spread(0)
    ways[0][1].wait_recv()
    project(3)
    ways[1][0].wait_recv()
    project(1)
    spread(3)
    spread(1)
    ways[0][2].wait_recv()
    ways[1][2].wait_recv()
    project(2)
    spread(2)

    order = [0, 3, 1, 2]
    acp = {}
    for r in order:
        hid = ys[r, y, 0].astype(F32)
        back = ys[r, y, 1].astype(F32)
        for d in range(1, NY):
            ycp[r, d].wait_recv()
            hid = hid + yr[r, d, 0].astype(F32)
            back = back + yr[r, d, 1].astype(F32)
        actf[r, core, y] = (back * gelu_slope(hid)).astype(BF16)
        for d in range(1, NY):
            cp = send(actf.at[r, core, y], actf.at[r, core, y], a_s.at[r, d - 1], a_r.at[r, d - 1], ydev[d])
            cp.start()
            acp[r, d] = cp
    accp = [send(actf.at[r, core], actf.at[r, core], ac_s.at[r], ac_r.at[r], other) for r in range(NX)]
    for r in order:
        for d in range(1, NY):
            acp[r, d].wait_recv()
        accp[r].start()

    gx = {
        1: send(part.at[1], xin.at[0], gx_s.at[0], gx_r.at[0], right),
        3: send(part.at[3], xin.at[1], gx_s.at[1], gx_r.at[1], left),
        "a": send(part.at[2, parts[0]], far.at[0], gx_s.at[2], gx_r.at[2], right),
        "b": send(part.at[2, parts[1]], far.at[1], gx_s.at[3], gx_r.at[3], left),
        "a2": send(far.at[0], far.at[2], gx_s.at[4], gx_r.at[4], right),
        "b2": send(far.at[1], far.at[3], gx_s.at[5], gx_r.at[5], left),
    }
    units = 2 * NY * rows

    def hidden_rows(r):
        return actf[r].reshape(units, 2 * tok)

    for r in [3, 1, 2, 0]:
        accp[r].wait()
        g = hidden_rows(r)
        half = units // 2
        value = dot(w1b[0], g[:half], 1, 0) + dot(w1b[1], g[half:], 1, 0)
        if r:
            for h in range(2):
                part[r, parts[h]] = value[:, h * tok:(h + 1) * tok].astype(BF16).reshape(nj, feat, tok)
            if r == 2:
                gx["a"].start()
                gx["b"].start()
            else:
                gx[r].start()
        else:
            own = value

    total = None
    for r in range(NX):
        term = dot(tokens(r, 0), hidden_rows(r)[:, :], 1, 1)
        total = term if total is None else total + term
    gx["a"].wait_recv()
    gx["a2"].start()
    gx["b"].wait_recv()
    gx["b2"].start()
    total = (total * scale).astype(BF16)
    width = wgs.shape[2]
    wgs[0] = total[:, :width]
    wgs[1] = total[:, width:]
    wcopy = send(wgs.at[1 - ylo], wgr, wg_s.at[0], wg_r.at[0], twin)
    wcopy.start()
    wg_out[half_rows, :] = wgs[ylo]

    gx[1].wait_recv()
    gx[3].wait_recv()
    gx["a2"].wait_recv()
    gx["b2"].wait_recv()
    for h in range(2):
        summed = own[:, h * tok:(h + 1) * tok].reshape(nj, feat, tok)
        summed = summed + xin[0, parts[h]].astype(F32) + xin[1, parts[h]].astype(F32) + far[2 + h].astype(F32)
        zs[parts[h]] = summed.astype(BF16)
    zz = []
    for d in range(1, nz):
        cp = send(zs.at[(z + d) % nz], zr.at[d], zz_s.at[d - 1], zz_r.at[d - 1], zdev[d])
        cp.start()
        zz.append(cp)
    result = zs[z].astype(F32)
    for d in range(1, nz):
        zz[d - 1].wait_recv()
        result = result + zr[d].astype(F32)
    fin[...] = result.astype(BF16)

    @pl.when(stays)
    def _():
        ig_out[...] = fin[...]

    @pl.when(jnp.logical_not(stays))
    def _():
        cp = send(fin, igr, p2_s.at[0], p2_r.at[0], origin)
        cp.start()
        cp.wait()
        ig_out[...] = igr[...]

    wcopy.wait()
    wg_out[other_rows, :] = wgr[...]
    for cp in zcp + zz + ways[0] + ways[1] + list(gx.values()) + list(ycp.values()) + list(acp.values()):
        cp.wait_send()


def body(inputs, out_grad, first_weight, second_weight):
    tok, feat = inputs.shape
    nz = lax.axis_size("mp") // (2 * NX)
    nj = nz // 2
    width = first_weight.shape[1]
    depth = nj * feat
    rows = width // NY
    scale = 1.0 / math.sqrt(tok * lax.axis_size("dp"))
    dma = pltpu.SemaphoreType.DMA
    vmem = pltpu.VMEM
    scratch = [
        vmem((NX, nz, 2, feat, tok), BF16),
        vmem((2, depth, width), BF16),
        vmem((2, width, depth), BF16),
        vmem((NX, 2, width, 2 * tok), F32),
        vmem((NX, 2, width, 2 * tok), F32),
        vmem((NX, 2, width, 2 * tok), F32),
        vmem((NX, NY, 2, rows, 2 * tok), BF16),
        vmem((NX, NY, 2, rows, 2 * tok), BF16),
        vmem((NX, NC, NY, rows, 2 * tok), BF16),
        vmem((NX, nz, feat, tok), BF16),
        vmem((2, nz, feat, tok), BF16),
        vmem((4, nj, feat, tok), BF16),
        vmem((nz, feat, tok), BF16),
        vmem((nz, feat, tok), BF16),
        vmem((feat, tok), BF16),
        vmem((feat, tok), BF16),
        vmem((2, depth, width), BF16),
        vmem((depth, width), BF16),
        dma((2,)), dma((2,)), dma((2,)), dma((2,)), dma((2,)),
        dma((nz - 1,)), dma((nz,)), dma((2, 3)), dma((2, 3)),
        dma((NX,)), dma((NX,)), dma((NX, NY - 1)), dma((NX, NY - 1)),
        dma((NX, NY - 1)), dma((NX, NY - 1)), dma((NX,)), dma((NX,)),
        dma((6,)), dma((6,)), dma((nz - 1,)), dma((nz - 1,)),
        dma((1,)), dma((1,)), dma((1,)), dma((1,)),
    ]
    ig, wg = pl.pallas_call(
        functools.partial(kernel, nz, scale),
        out_shape=(jax.ShapeDtypeStruct((feat, tok), BF16),
                   jax.ShapeDtypeStruct(first_weight.shape, BF16)),
        in_specs=[pl.BlockSpec(memory_space=pl.ANY)] * 4,
        out_specs=(pl.BlockSpec(memory_space=pltpu.VMEM),) * 2,
        scratch_shapes=scratch,
        compiler_params=pltpu.CompilerParams(
            collective_id=0, has_side_effects=True, vmem_limit_bytes=40 * 2 ** 20),
        name="block_backward",
    )(inputs.T, out_grad.T, first_weight, second_weight)
    return (ig.T, wg)


def solution(mesh):
    return jax.shard_map(
        body,
        mesh=mesh,
        in_specs=(P("dp", "mp"), P("dp", "mp"), P("dp", "mp"), P("mp", "dp")),
        out_specs=(P("dp", "mp"), P("dp", "mp")),
        check_vma=False,
    )
```

```python
import functools
import math

import jax
import jax.numpy as jnp
from jax import lax
from jax.experimental import pallas as pl
from jax.experimental.pallas import tpu as pltpu
from jax.sharding import PartitionSpec as P

NX, NY, NC = 4, 8, 2
F32, BF16 = jnp.float32, jnp.bfloat16
ROOT_HALF, ROOT_TWO_PI = math.sqrt(0.5), math.sqrt(2.0 * math.pi)


def gelu_slope(v):
    cdf = 0.5 * (1.0 + lax.erf(v * ROOT_HALF))
    return cdf + v * jnp.exp(-0.5 * v * v) / ROOT_TWO_PI


def dot(a, b, ca, cb):
    return lax.dot_general(a, b, (((ca,), (cb,)), ((), ())), preferred_element_type=F32)


def kernel(nz, scale, xt, gt, w1, w2, ig_out, wg_out,
           buf, w1b, w1t, w2b, cs, cr, keep, ys, yr, actf, part, xin, zs, zr, fin, igr, wgs, wgr,
           loc, w_s, w_r, p_s, p_r, x_s, x_r, c_s, c_r, y_s, y_r, a_s, a_r, ac_s, ac_r,
           gx_s, gx_r, zz_s, zz_r, p2_s, p2_r, wg_s, wg_r):
    nj = nz // 2
    feat, tok = xt.shape
    depth = nj * feat
    col = nz * NX
    rows = ys.shape[3]
    dp, mp = lax.axis_index("dp"), lax.axis_index("mp")
    core, ylo = dp % 2, mp // col
    z, x = (mp % col) // NX, mp % NX
    y = (dp // 2) * 2 + ylo
    pending = []

    def at(x_, y_, z_, c_):
        return ((y_ // 2) * 2 + c_, (y_ % 2) * col + z_ * NX + x_)

    def copy(src, dst, ssem, rsem, dev):
        return pltpu.make_async_remote_copy(
            src_ref=src, dst_ref=dst, send_sem=ssem, recv_sem=rsem,
            device_id=dev, device_id_type=pl.DeviceIdType.MESH)

    def send(*args):
        cp = copy(*args)
        cp.start()
        pending.append(cp)
        return cp

    xdev = [at((x + d) % NX, y, z, core) for d in range(NX)]
    other = at(x, y, z, 1 - core)
    twin = at(x, y + 1 - 2 * ylo, z, core)
    ydev = [at(x, (y + d) % NY, z, core) for d in range(NY)]
    zdev = [at(x, y, (z + d) % nz, core) for d in range(nz)]
    plane = mp // nj
    slot = (dp // NX) * nj + mp % nj
    goals = [(plane // 2, (plane % 2) * col + ((z + t) % nz) * NX + dp % NX) for t in range(nz)]
    here = jnp.logical_and(jnp.logical_and(plane // 2 == dp, plane % 2 == ylo), dp % NX == x)
    stays = jnp.logical_and(here, slot == z)

    def owner(s):
        return ((s // nj) * NX + x, (dp * 2 + ylo) * nj + s % nj)

    def unless(condition, action):
        pl.when(jnp.logical_not(condition))(action)

    half_rows = pl.ds(pl.multiple_of(ylo * depth, 128), depth)
    other_rows = pl.ds(pl.multiple_of((1 - ylo) * depth, 128), depth)
    lw1 = pltpu.make_async_copy(w1.at[half_rows, :], w1b.at[ylo], loc.at[0])
    lw2 = pltpu.make_async_copy(w2.at[:, half_rows], w2b.at[ylo], loc.at[1])
    lw1.start()
    lw2.start()

    barrier = pltpu.get_barrier_semaphore()

    def greet(dev):
        pl.semaphore_signal(barrier, inc=1, device_id=dev, device_id_type=pl.DeviceIdType.MESH)

    for s in range(nz):
        unless(jnp.logical_and(here, slot == s), functools.partial(greet, owner(s)))
    unless(stays, lambda: greet((goals[0][0], (plane % 2) * col + slot * NX + dp % NX)))
    for dev in xdev[1:] + [other] + ydev[1:] + zdev[1:]:
        greet(dev)
    peers = (NX - 1) + 1 + (NY - 1) + (nz - 1) + nz + 1
    pl.semaphore_wait(barrier, peers - jnp.where(here, 1, 0) - jnp.where(stays, 1, 0))
    sources = [xt, gt]
    spots = [nz // 2] + [d for i in range(1, nz // 2) for d in (nz // 2 - i, nz // 2 + i)]

    def p_copy(w, t):
        return copy(sources[w], buf.at[w, 0, slot], p_s.at[w, t], p_r.at[w, slot], goals[t])

    def p_local(w):
        return pltpu.make_async_copy(sources[w], buf.at[w, 0, slot], loc.at[2 + w])

    for w in range(2):
        for t in spots:
            cp = p_copy(w, t)
            cp.start()
            pending.append(cp)
        pl.when(here)(p_local(w).start)
        unless(here, p_copy(w, 0).start)
    wcp = [send(w1.at[other_rows, :], w1b.at[ylo], w_s.at[0], w_r.at[0], twin),
           send(w2.at[:, other_rows], w2b.at[ylo], w_s.at[1], w_r.at[1], twin)]
    for w in range(2):
        pl.when(here)(p_local(w).wait)
    halves = [pl.ds(0, nj), pl.ds(nj, nj)]

    def x_copy(w, h, d):
        return copy(buf.at[w, 0, halves[h]], buf.at[w, NX - d, halves[h]],
                    x_s.at[w, h, d - 1], x_r.at[w, h, d - 1], xdev[d])

    def along_x(w, h):
        for s in range(h * nj, h * nj + nj):
            unless(jnp.logical_and(here, slot == s),
                   copy(sources[w], buf.at[w, 0, s], p_s.at[w, 0], p_r.at[w, s], goals[0]).wait_recv)
        for d in (2, 1, 3):
            cp = x_copy(w, h, d)
            cp.start()
            pending.append(cp)

    def tokens(w, h):
        return jnp.concatenate(
            [buf[w, r, h * nj:(h + 1) * nj].reshape(depth, tok) for r in range(NX)], axis=1)

    weight = [w1t, w2b]

    def c_copy(w, h):
        return copy(cs.at[w, h], cr.at[w, h], c_s.at[w, h], c_r.at[w, h], other)

    def project(w, h):
        for d in (1, 3, 2):
            x_copy(w, h, d).wait_recv()
        t = tokens(w, h)
        cs[w, h] = dot(weight[w][1 - core], t, 1, 0)
        cp = c_copy(w, h)
        cp.start()
        pending.append(cp)
        keep[w, h] = dot(weight[w][core], t, 1, 0)

    def y_copy(w, h, d):
        return copy(ys.at[w, h, (y + d) % NY], yr.at[w, h, d], y_s.at[w, h, d - 1], y_r.at[w, h, d - 1], ydev[d])

    def spread(w, h):
        c_copy(w, h).wait_recv()
        ys[w, h] = (keep[w, h] + cr[w, h]).astype(BF16).reshape(NY, rows, NX * tok)
        for d in (4, 3, 5, 2, 6, 1, 7):
            cp = y_copy(w, h, d)
            cp.start()
            pending.append(cp)

    along_x(0, 0)
    along_x(0, 1)
    lw1.wait()
    wcp[0].wait_recv()
    for i in range(2):
        w1t[i] = w1b[i].T
    lw2.wait()
    wcp[1].wait_recv()
    along_x(1, 0)
    project(0, 0)
    along_x(1, 1)
    project(0, 1)
    spread(0, 0)
    project(1, 0)
    spread(0, 1)
    spread(1, 0)
    project(1, 1)
    spread(1, 1)

    def a_copy(h, d):
        return copy(actf.at[h, core, y], actf.at[h, core, y], a_s.at[h, d - 1], a_r.at[h, d - 1], ydev[d])

    def act(h):
        sums = []
        for w in range(2):
            total = ys[w, h, y].astype(F32)
            for d in range(1, NY):
                y_copy(w, h, d).wait_recv()
                total = total + yr[w, h, d].astype(F32)
            sums.append(total)
        actf[h, core, y] = (sums[1] * gelu_slope(sums[0])).astype(BF16)
        for d in (4, 3, 5, 2, 6, 1, 7):
            cp = a_copy(h, d)
            cp.start()
            pending.append(cp)

    def ac_copy(h):
        return copy(actf.at[h, core], actf.at[h, core], ac_s.at[h], ac_r.at[h], other)

    def to_other(h):
        for d in range(1, NY):
            a_copy(h, d).wait_recv()
        cp = ac_copy(h)
        cp.start()
        pending.append(cp)

    def hidden_rows(h):
        return actf[h].reshape(NC * NY * rows, NX * tok)

    def g_copy(h, r):
        return copy(part.at[r, halves[h]], xin.at[r, halves[h]], gx_s.at[h, r - 1], gx_r.at[h, r - 1], xdev[r])

    def back_to_features(h):
        ac_copy(h).wait_recv()
        g = hidden_rows(h)
        half = NY * rows
        value = dot(w1b[0], g[:half], 1, 0) + dot(w1b[1], g[half:], 1, 0)
        for r in (2, 1, 3):
            part[r, halves[h]] = value[:, r * tok:(r + 1) * tok].astype(BF16).reshape(nj, feat, tok)
            cp = g_copy(h, r)
            cp.start()
            pending.append(cp)
        return value[:, :tok]

    def zz_copy(d):
        return copy(zs.at[(z + d) % nz], zr.at[d], zz_s.at[d - 1], zz_r.at[d - 1], zdev[d])

    def along_z(h, own):
        summed = own.reshape(nj, feat, tok)
        for r in (1, 3, 2):
            g_copy(h, r).wait_recv()
            summed = summed + xin[r, halves[h]].astype(F32)
        zs[halves[h]] = summed.astype(BF16)
        for t in range(h * nj, h * nj + nj):
            d = (t - z + nz) % nz
            unless(t == z, copy(zs.at[t], zr.at[d], zz_s.at[d - 1], zz_r.at[d - 1],
                                (dp, ylo * col + t * NX + x)).start)

    act(0)
    act(1)
    to_other(0)
    own = [back_to_features(0)]
    to_other(1)
    own.append(back_to_features(1))
    along_z(0, own[0])

    total = (dot(tokens(0, 0), hidden_rows(0), 1, 1) + dot(tokens(0, 1), hidden_rows(1), 1, 1)) * scale
    width = wgs.shape[2]
    for i in range(2):
        wgs[i] = total[:, i * width:(i + 1) * width].astype(BF16)
    wcopy = send(wgs.at[1 - ylo], wgr, wg_s.at[0], wg_r.at[0], twin)
    wg_out[half_rows, :] = wgs[ylo]

    along_z(1, own[1])
    result = zs[z].astype(F32)
    for d in range(1, nz):
        zz_copy(d).wait_recv()
        result = result + zr[d].astype(F32)
    fin[...] = result.astype(BF16)

    @pl.when(stays)
    def _():
        ig_out[...] = fin[...]

    @pl.when(jnp.logical_not(stays))
    def _():
        cp = copy(fin, igr, p2_s.at[0], p2_r.at[0], owner(z))
        cp.start()
        cp.wait()
        ig_out[...] = igr[...]

    wcopy.wait_recv()
    wg_out[other_rows, :] = wgr[...]
    for w in range(2):
        unless(here, p_copy(w, 0).wait_send)
    for d in range(1, nz):
        zz_copy(d).wait_send()
    for cp in pending:
        cp.wait_send()


def body(inputs, out_grad, first_weight, second_weight):
    tok, feat = inputs.shape
    nz = lax.axis_size("mp") // (2 * NX)
    nj = nz // 2
    width = first_weight.shape[1]
    depth = nj * feat
    rows = width // NY
    scale = 1.0 / math.sqrt(tok * lax.axis_size("dp"))
    dma = pltpu.SemaphoreType.DMA
    vmem = pltpu.VMEM
    scratch = [
        vmem((2, NX, nz, feat, tok), BF16),
        vmem((2, depth, width), BF16),
        vmem((2, width, depth), BF16),
        vmem((2, width, depth), BF16),
        vmem((2, 2, width, NX * tok), F32),
        vmem((2, 2, width, NX * tok), F32),
        vmem((2, 2, width, NX * tok), F32),
        vmem((2, 2, NY, rows, NX * tok), BF16),
        vmem((2, 2, NY, rows, NX * tok), BF16),
        vmem((2, NC, NY, rows, NX * tok), BF16),
        vmem((NX, nz, feat, tok), BF16),
        vmem((NX, nz, feat, tok), BF16),
        vmem((nz, feat, tok), BF16),
        vmem((nz, feat, tok), BF16),
        vmem((feat, tok), BF16),
        vmem((feat, tok), BF16),
        vmem((2, depth, width), BF16),
        vmem((depth, width), BF16),
        dma((4,)), dma((2,)), dma((2,)), dma((2, nz)), dma((2, nz)),
        dma((2, 2, NX - 1)), dma((2, 2, NX - 1)), dma((2, 2)), dma((2, 2)),
        dma((2, 2, NY - 1)), dma((2, 2, NY - 1)), dma((2, NY - 1)), dma((2, NY - 1)),
        dma((2,)), dma((2,)), dma((2, NX - 1)), dma((2, NX - 1)), dma((nz - 1,)), dma((nz - 1,)),
        dma((1,)), dma((1,)), dma((1,)), dma((1,)),
    ]
    ig, wg = pl.pallas_call(
        functools.partial(kernel, nz, scale),
        out_shape=(jax.ShapeDtypeStruct((feat, tok), BF16),
                   jax.ShapeDtypeStruct(first_weight.shape, BF16)),
        in_specs=[pl.BlockSpec(memory_space=pl.ANY)] * 4,
        out_specs=(pl.BlockSpec(memory_space=pltpu.VMEM),) * 2,
        scratch_shapes=scratch,
        compiler_params=pltpu.CompilerParams(
            collective_id=0, has_side_effects=True, vmem_limit_bytes=62 * 2 ** 20),
        name="block_backward",
    )(inputs.T, out_grad.T, first_weight, second_weight)
    return (ig.T, wg)


def solution(mesh):
    return jax.shard_map(
        body,
        mesh=mesh,
        in_specs=(P("dp", "mp"), P("dp", "mp"), P("dp", "mp"), P("mp", "dp")),
        out_specs=(P("dp", "mp"), P("dp", "mp")),
        check_vma=False,
    )
```

```python
import functools
import math

import jax
import jax.numpy as jnp
from jax import lax
from jax.experimental import pallas as pl
from jax.experimental.pallas import tpu as pltpu
from jax.sharding import PartitionSpec as P

NX, NY, NC = 4, 8, 2
ORDER = (0, 2, 1, 3)
X_STEPS, Y_STEPS = (2, 1, 3), (4, 3, 5, 2, 6, 1, 7)
CHUNKS = ((0, 0, 4), (1, 0, 4))
F32, BF16 = jnp.float32, jnp.bfloat16
ROOT_HALF, ROOT_TWO_PI = math.sqrt(0.5), math.sqrt(2.0 * math.pi)


def gelu_slope(v):
    cdf = 0.5 * (1.0 + lax.erf(v * ROOT_HALF))
    return cdf + v * jnp.exp(-0.5 * v * v) / ROOT_TWO_PI


def dot(a, b, ca, cb):
    return lax.dot_general(a, b, (((ca,), (cb,)), ((), ())), preferred_element_type=F32)


def kernel(nz, scale, xt, gt, w1, w2, ig_out, wg_out,
           buf, u, w1b, w1t, w2b, cs, cr, keep, ys, yr, actf, part, xin, zs, zr, fin, igr, wgs, wgr,
           loc, w_s, w_r, p_s, p_r, x_s, x_r, c_s, c_r, y_s, y_r, a_s, a_r, ac_s, ac_r,
           gx_s, gx_r, zz_s, zz_r, p2_s, p2_r, wg_s, wg_r):
    nj = nz // 2
    feat, tok = xt.shape
    depth = nj * feat
    col = nz * NX
    rows = ys.shape[3]
    dp, mp = lax.axis_index("dp"), lax.axis_index("mp")
    core, ylo = dp % 2, mp // col
    z, x = (mp % col) // NX, mp % NX
    y = (dp // 2) * 2 + ylo
    pending = []

    def at(x_, y_, z_, c_):
        return ((y_ // 2) * 2 + c_, (y_ % 2) * col + z_ * NX + x_)

    def copy(src, dst, ssem, rsem, dev):
        return pltpu.make_async_remote_copy(
            src_ref=src, dst_ref=dst, send_sem=ssem, recv_sem=rsem,
            device_id=dev, device_id_type=pl.DeviceIdType.MESH)

    def send(*args):
        cp = copy(*args)
        cp.start()
        pending.append(cp)
        return cp

    xdev = [at((x + d) % NX, y, z, core) for d in range(NX)]
    other = at(x, y, z, 1 - core)
    twin = at(x, y + 1 - 2 * ylo, z, core)
    ydev = [at(x, (y + d) % NY, z, core) for d in range(NY)]
    zdev = [at(x, y, (z + d) % nz, core) for d in range(nz)]
    plane = mp // nj
    slot = (dp // NX) * nj + mp % nj
    goals = [(plane // 2, (plane % 2) * col + t * NX + dp % NX) for t in range(nz)]
    here = jnp.logical_and(jnp.logical_and(plane // 2 == dp, plane % 2 == ylo), dp % NX == x)
    stays = jnp.logical_and(here, slot == z)

    def owner(s):
        return ((s // nj) * NX + x, (dp * 2 + ylo) * nj + s % nj)

    def unless(condition, action):
        pl.when(jnp.logical_not(condition))(action)

    half_rows = pl.ds(pl.multiple_of(ylo * depth, 128), depth)
    other_rows = pl.ds(pl.multiple_of((1 - ylo) * depth, 128), depth)
    lu = [pltpu.make_async_copy(xt, u.at[0], loc.at[4]), pltpu.make_async_copy(gt, u.at[1], loc.at[5])]
    for cp in lu:
        cp.start()
    lw1 = pltpu.make_async_copy(w1.at[half_rows, :], w1b.at[ylo], loc.at[0])
    lw2 = pltpu.make_async_copy(w2.at[:, half_rows], w2b.at[ylo], loc.at[1])
    lw1.start()
    lw2.start()

    barrier = pltpu.get_barrier_semaphore()

    def greet(dev):
        pl.semaphore_signal(barrier, inc=1, device_id=dev, device_id_type=pl.DeviceIdType.MESH)

    for s in range(nz):
        unless(jnp.logical_and(here, slot == s), functools.partial(greet, owner(s)))
    unless(stays, lambda: greet((goals[0][0], (plane % 2) * col + slot * NX + dp % NX)))
    for dev in xdev[1:] + [other] + ydev[1:] + zdev[1:]:
        greet(dev)
    peers = (NX - 1) + 1 + (NY - 1) + (nz - 1) + nz + 1
    pl.semaphore_wait(barrier, peers - jnp.where(here, 1, 0) - jnp.where(stays, 1, 0))
    sources = [u.at[0], u.at[1]]
    for cp in lu:
        cp.wait()

    def p_copy(w, t):
        return copy(sources[w], buf.at[w, 0, slot], p_s.at[w, t], p_r.at[w, slot], goals[t])

    def p_local(w):
        return pltpu.make_async_copy(sources[w], buf.at[w, 0, slot], loc.at[2 + w])

    for w in range(2):
        for t in range(nz):
            unless(jnp.logical_and(here, z == t), p_copy(w, t).start)
        pl.when(here)(p_local(w).start)
    wcp = [send(w1.at[other_rows, :], w1b.at[ylo], w_s.at[0], w_r.at[0], twin),
           send(w2.at[:, other_rows], w2b.at[ylo], w_s.at[1], w_r.at[1], twin)]
    for w in range(2):
        pl.when(here)(p_local(w).wait)
    halves = [pl.ds(0, nj), pl.ds(nj, nj)]

    def x_copy(w, h, d):
        return copy(buf.at[w, 0, halves[h]], buf.at[w, NX - d, halves[h]],
                    x_s.at[w, h, d - 1], x_r.at[w, h, d - 1], xdev[d])

    def begin(cp):
        cp.start()
        pending.append(cp)

    def along_x(w, h):
        for s in range(h * nj, h * nj + nj):
            unless(jnp.logical_and(here, slot == s),
                   copy(sources[w], buf.at[w, 0, s], p_s.at[w, 0], p_r.at[w, s], goals[0]).wait_recv)
        for d in X_STEPS:
            begin(x_copy(w, h, d))

    def arrived(w, h, r):
        if r:
            x_copy(w, h, NX - r).wait_recv()

    whole = [(0, 0, NX), (1, 0, NX)]
    chunks = [whole, CHUNKS]

    def lanes(chunk):
        return pl.ds(chunk[1] * tok, (chunk[2] - chunk[1]) * tok)

    def tokens(w, chunk):
        h, lo, hi = chunk
        return jnp.concatenate(
            [buf[w, ORDER[i], h * nj:(h + 1) * nj].reshape(depth, tok) for i in range(lo, hi)], axis=1)

    weight = [w1t, w2b]

    def c_copy(w, i):
        h = chunks[w][i][0]
        part_ = lanes(chunks[w][i])
        return copy(cs.at[w, h, :, part_], cr.at[w, h, :, part_], c_s.at[w, i], c_r.at[w, i], other)

    def project(w, i):
        h, lo, hi = chunks[w][i]
        for place in range(lo, hi):
            arrived(w, h, ORDER[place])
        t = tokens(w, chunks[w][i])
        cs[w, h, :, lo * tok:hi * tok] = dot(weight[w][1 - core], t, 1, 0)
        begin(c_copy(w, i))
        keep[w, h, :, lo * tok:hi * tok] = dot(weight[w][core], t, 1, 0)

    def y_copy(w, i, d):
        h, part_ = chunks[w][i][0], lanes(chunks[w][i])
        return copy(ys.at[w, h, (y + d) % NY, :, part_], yr.at[w, h, d, :, part_],
                    y_s.at[w, i, d - 1], y_r.at[w, i, d - 1], ydev[d])

    def spread(w, i):
        h, lo, hi = chunks[w][i]
        c_copy(w, i).wait_recv()
        total = keep[w, h, :, lo * tok:hi * tok] + cr[w, h, :, lo * tok:hi * tok]
        ys[w, h, :, :, lo * tok:hi * tok] = total.astype(BF16).reshape(NY, rows, (hi - lo) * tok)
        for d in Y_STEPS:
            begin(y_copy(w, i, d))
    along_x(0, 0)
    along_x(0, 1)
    along_x(1, 0)
    along_x(1, 1)
    lw1.wait()
    wcp[0].wait_recv()
    for i in range(2):
        w1t[i] = w1b[i].T
    lw2.wait()
    wcp[1].wait_recv()
    project(0, 0)
    project(0, 1)
    spread(0, 0)
    spread(0, 1)
    project(1, 0)
    spread(1, 0)
    for i in range(1, len(CHUNKS)):
        project(1, i)
    for i in range(1, len(CHUNKS)):
        spread(1, i)

    def a_copy(i, d):
        h, part_ = CHUNKS[i][0], lanes(CHUNKS[i])
        return copy(actf.at[h, core, y, :, part_], actf.at[h, core, y, :, part_],
                    a_s.at[i, d - 1], a_r.at[i, d - 1], ydev[d])

    def act(i):
        h, lo, hi = CHUNKS[i]
        sums = []
        for w in range(2):
            total = ys[w, h, y, :, lo * tok:hi * tok].astype(F32)
            for d in range(1, NY):
                if w == 1:
                    y_copy(w, i, d).wait_recv()
                elif lo == 0:
                    y_copy(w, h, d).wait_recv()
                total = total + yr[w, h, d, :, lo * tok:hi * tok].astype(F32)
            sums.append(total)
        actf[h, core, y, :, lo * tok:hi * tok] = (sums[1] * gelu_slope(sums[0])).astype(BF16)
        for d in Y_STEPS:
            begin(a_copy(i, d))

    def ac_copy(i):
        h, part_ = CHUNKS[i][0], lanes(CHUNKS[i])
        return copy(actf.at[h, core, :, :, part_], actf.at[h, core, :, :, part_], ac_s.at[i], ac_r.at[i], other)

    def to_other(i):
        for d in range(1, NY):
            a_copy(i, d).wait_recv()
        begin(ac_copy(i))

    def hidden_rows(chunk):
        h, lo, hi = chunk
        return actf[h, :, :, :, lo * tok:hi * tok].reshape(NC * NY * rows, (hi - lo) * tok)

    def g_copy(h, r):
        return copy(part.at[r, halves[h]], xin.at[r, halves[h]], gx_s.at[h, r - 1], gx_r.at[h, r - 1], xdev[r])

    own = {}

    def back_to_features(i):
        h, lo, hi = CHUNKS[i]
        ac_copy(i).wait_recv()
        g = hidden_rows(CHUNKS[i])
        half = NY * rows
        value = dot(w1b[0], g[:half], 1, 0) + dot(w1b[1], g[half:], 1, 0)
        for place in range(hi - 1, lo - 1, -1):
            r = ORDER[place]
            this = value[:, (place - lo) * tok:(place - lo + 1) * tok]
            if r == 0:
                own[h] = this
            else:
                part[r, halves[h]] = this.astype(BF16).reshape(nj, feat, tok)
                begin(g_copy(h, r))

    def zz_copy(d):
        return copy(zs.at[(z + d) % nz], zr.at[d], zz_s.at[d - 1], zz_r.at[d - 1], zdev[d])

    def along_z(h, own):
        summed = own.reshape(nj, feat, tok)
        for r in (1, 3, 2):
            g_copy(h, r).wait_recv()
            summed = summed + xin[r, halves[h]].astype(F32)
        zs[halves[h]] = summed.astype(BF16)
        for t in range(h * nj, h * nj + nj):
            d = (t - z + nz) % nz
            unless(t == z, copy(zs.at[t], zr.at[d], zz_s.at[d - 1], zz_r.at[d - 1],
                                (dp, ylo * col + t * NX + x)).start)
    for i in range(len(CHUNKS)):
        act(i)
    to_other(0)
    back_to_features(0)
    for i in range(1, len(CHUNKS)):
        to_other(i)
        back_to_features(i)
    along_z(0, own[0])

    total = sum(dot(tokens(0, c), hidden_rows(c), 1, 1) for c in whole) * scale
    width = wgs.shape[2]
    for i in range(2):
        wgs[i] = total[:, i * width:(i + 1) * width].astype(BF16)
    wcopy = send(wgs.at[1 - ylo], wgr, wg_s.at[0], wg_r.at[0], twin)
    wg_out[half_rows, :] = wgs[ylo]

    along_z(1, own[1])
    result = zs[z].astype(F32)
    for d in range(1, nz):
        zz_copy(d).wait_recv()
        result = result + zr[d].astype(F32)
    fin[...] = result.astype(BF16)

    @pl.when(stays)
    def _():
        ig_out[...] = fin[...]

    @pl.when(jnp.logical_not(stays))
    def _():
        cp = copy(fin, igr, p2_s.at[0], p2_r.at[0], owner(z))
        cp.start()
        cp.wait()
        ig_out[...] = igr[...]

    wcopy.wait_recv()
    wg_out[other_rows, :] = wgr[...]
    for w in range(2):
        for t in range(nz):
            unless(jnp.logical_and(here, z == t), p_copy(w, t).wait_send)
    for d in range(1, nz):
        zz_copy(d).wait_send()
    for cp in pending:
        cp.wait_send()


def body(inputs, out_grad, first_weight, second_weight):
    tok, feat = inputs.shape
    nz = lax.axis_size("mp") // (2 * NX)
    nj = nz // 2
    width = first_weight.shape[1]
    depth = nj * feat
    rows = width // NY
    scale = 1.0 / math.sqrt(tok * lax.axis_size("dp"))
    dma = pltpu.SemaphoreType.DMA
    vmem = pltpu.VMEM
    scratch = [
        vmem((2, NX, nz, feat, tok), BF16),
        vmem((2, feat, tok), BF16),
        vmem((2, depth, width), BF16),
        vmem((2, width, depth), BF16),
        vmem((2, width, depth), BF16),
        vmem((2, 2, width, NX * tok), F32),
        vmem((2, 2, width, NX * tok), F32),
        vmem((2, 2, width, NX * tok), F32),
        vmem((2, 2, NY, rows, NX * tok), BF16),
        vmem((2, 2, NY, rows, NX * tok), BF16),
        vmem((2, NC, NY, rows, NX * tok), BF16),
        vmem((NX, nz, feat, tok), BF16),
        vmem((NX, nz, feat, tok), BF16),
        vmem((nz, feat, tok), BF16),
        vmem((nz, feat, tok), BF16),
        vmem((feat, tok), BF16),
        vmem((feat, tok), BF16),
        vmem((2, depth, width), BF16),
        vmem((depth, width), BF16),
        dma((6,)), dma((2,)), dma((2,)), dma((2, nz)), dma((2, nz)),
        dma((2, 2, NX - 1)), dma((2, 2, NX - 1)), dma((2, 3)), dma((2, 3)),
        dma((2, 3, NY - 1)), dma((2, 3, NY - 1)), dma((3, NY - 1)), dma((3, NY - 1)),
        dma((3,)), dma((3,)), dma((2, NX - 1)), dma((2, NX - 1)), dma((nz - 1,)), dma((nz - 1,)),
        dma((1,)), dma((1,)), dma((1,)), dma((1,)),
    ]
    ig, wg = pl.pallas_call(
        functools.partial(kernel, nz, scale),
        out_shape=(jax.ShapeDtypeStruct((feat, tok), BF16),
                   jax.ShapeDtypeStruct(first_weight.shape, BF16)),
        in_specs=[pl.BlockSpec(memory_space=pl.ANY)] * 4,
        out_specs=(pl.BlockSpec(memory_space=pltpu.VMEM),) * 2,
        scratch_shapes=scratch,
        compiler_params=pltpu.CompilerParams(
            collective_id=0, has_side_effects=True, vmem_limit_bytes=62 * 2 ** 20),
        name="block_backward",
    )(inputs.T, out_grad.T, first_weight, second_weight)
    return (ig.T, wg)


def solution(mesh):
    return jax.shard_map(
        body,
        mesh=mesh,
        in_specs=(P("dp", "mp"), P("dp", "mp"), P("dp", "mp"), P("mp", "dp")),
        out_specs=(P("dp", "mp"), P("dp", "mp")),
        check_vma=False,
    )
```

```python
import functools
import math

import jax
import jax.numpy as jnp
from jax import lax
from jax.experimental import pallas as pl
from jax.experimental.pallas import tpu as pltpu
from jax.sharding import PartitionSpec as P

NX, NY, NC = 4, 8, 2
ORDER = (0, 2, 1, 3)
X_STEPS, Y_STEPS = (2, 1, 3), (4, 3, 5, 2, 6, 1, 7)
CHUNKS = ((0, 0, 4), (1, 0, 4))
F32, BF16 = jnp.float32, jnp.bfloat16
ROOT_HALF, ROOT_TWO_PI = math.sqrt(0.5), math.sqrt(2.0 * math.pi)


def gelu_slope(v):
    cdf = 0.5 * (1.0 + lax.erf(v * ROOT_HALF))
    return cdf + v * jnp.exp(-0.5 * v * v) / ROOT_TWO_PI


def dot(a, b, ca, cb):
    return lax.dot_general(a, b, (((ca,), (cb,)), ((), ())), preferred_element_type=F32)


def kernel(nz, scale, xt, gt, w1, w2, ig_out, wg_out,
           buf, u, w1b, w1t, w2b, cs, cr, keep, ys, yr, actf, part, xin, zs, zr, fin, igr, wgs, wgr,
           loc, w_s, w_r, p_s, p_r, x_s, x_r, c_s, c_r, y_s, y_r, a_s, a_r, ac_s, ac_r,
           gx_s, gx_r, zz_s, zz_r, p2_s, p2_r, wg_s, wg_r):
    nj = nz // 2
    feat, tok = xt.shape
    depth = nj * feat
    col = nz * NX
    rows = ys.shape[3]
    dp, mp = lax.axis_index("dp"), lax.axis_index("mp")
    core, ylo = dp % 2, mp // col
    z, x = (mp % col) // NX, mp % NX
    y = (dp // 2) * 2 + ylo
    pending = []

    def at(x_, y_, z_, c_):
        return ((y_ // 2) * 2 + c_, (y_ % 2) * col + z_ * NX + x_)

    def copy(src, dst, ssem, rsem, dev):
        return pltpu.make_async_remote_copy(
            src_ref=src, dst_ref=dst, send_sem=ssem, recv_sem=rsem,
            device_id=dev, device_id_type=pl.DeviceIdType.MESH)

    def send(*args):
        cp = copy(*args)
        cp.start()
        pending.append(cp)
        return cp

    xdev = [at((x + d) % NX, y, z, core) for d in range(NX)]
    other = at(x, y, z, 1 - core)
    twin = at(x, y + 1 - 2 * ylo, z, core)
    ydev = [at(x, (y + d) % NY, z, core) for d in range(NY)]
    zdev = [at(x, y, (z + d) % nz, core) for d in range(nz)]
    plane = mp // nj
    slot = (dp // NX) * nj + mp % nj
    goals = [(plane // 2, (plane % 2) * col + t * NX + dp % NX) for t in range(nz)]
    here = jnp.logical_and(jnp.logical_and(plane // 2 == dp, plane % 2 == ylo), dp % NX == x)
    stays = jnp.logical_and(here, slot == z)

    def owner(s):
        return ((s // nj) * NX + x, (dp * 2 + ylo) * nj + s % nj)

    def unless(condition, action):
        pl.when(jnp.logical_not(condition))(action)

    half_rows = pl.ds(pl.multiple_of(ylo * depth, 128), depth)
    other_rows = pl.ds(pl.multiple_of((1 - ylo) * depth, 128), depth)
    lu = [pltpu.make_async_copy(xt, u.at[0], loc.at[4]), pltpu.make_async_copy(gt, u.at[1], loc.at[5])]
    for cp in lu:
        cp.start()
    lw1 = pltpu.make_async_copy(w1.at[half_rows, :], w1b.at[ylo], loc.at[0])
    lw2 = pltpu.make_async_copy(w2.at[:, half_rows], w2b.at[ylo], loc.at[1])
    lw1.start()
    lw2.start()

    barrier = pltpu.get_barrier_semaphore()

    def greet(dev):
        pl.semaphore_signal(barrier, inc=1, device_id=dev, device_id_type=pl.DeviceIdType.MESH)

    for s in range(nz):
        unless(jnp.logical_and(here, slot == s), functools.partial(greet, owner(s)))
    unless(stays, lambda: greet((goals[0][0], (plane % 2) * col + slot * NX + dp % NX)))
    for dev in xdev[1:] + [other] + ydev[1:] + zdev[1:]:
        greet(dev)
    peers = (NX - 1) + 1 + (NY - 1) + (nz - 1) + nz + 1
    pl.semaphore_wait(barrier, peers - jnp.where(here, 1, 0) - jnp.where(stays, 1, 0))
    sources = [u.at[0], u.at[1]]
    for cp in lu:
        cp.wait()

    def p_copy(w, t):
        return copy(sources[w], buf.at[w, 0, slot], p_s.at[w, t], p_r.at[w, slot], goals[t])

    def p_local(w):
        return pltpu.make_async_copy(sources[w], buf.at[w, 0, slot], loc.at[2 + w])

    for w in range(2):
        for t in range(nz):
            unless(jnp.logical_and(here, z == t), p_copy(w, t).start)
        pl.when(here)(p_local(w).start)
    wcp = [send(w1.at[other_rows, :], w1b.at[ylo], w_s.at[0], w_r.at[0], twin),
           send(w2.at[:, other_rows], w2b.at[ylo], w_s.at[1], w_r.at[1], twin)]
    for w in range(2):
        pl.when(here)(p_local(w).wait)
    halves = [pl.ds(0, nj), pl.ds(nj, nj)]

    runs = [[(h * nj, nj // 2), (h * nj + nj // 2, nj - nj // 2)] for h in range(2)]

    def x_copy(w, h, k, d):
        span = pl.ds(*runs[h][k])
        return copy(buf.at[w, 0, span], buf.at[w, NX - d, span],
                    x_s.at[w, h, k, d - 1], x_r.at[w, h, k, d - 1], xdev[d])

    def begin(cp):
        cp.start()
        pending.append(cp)

    def along_x(w, h):
        for k, (first, count) in enumerate(runs[h]):
            for s in range(first, first + count):
                unless(jnp.logical_and(here, slot == s),
                       copy(sources[w], buf.at[w, 0, s], p_s.at[w, 0], p_r.at[w, s], goals[0]).wait_recv)
            for d in X_STEPS:
                begin(x_copy(w, h, k, d))

    def arrived(w, h, r):
        if r:
            for k in range(2):
                x_copy(w, h, k, NX - r).wait_recv()

    whole = [(0, 0, NX), (1, 0, NX)]
    chunks = [whole, CHUNKS]

    def lanes(chunk):
        return pl.ds(chunk[1] * tok, (chunk[2] - chunk[1]) * tok)

    def tokens(w, chunk):
        h, lo, hi = chunk
        return jnp.concatenate(
            [buf[w, ORDER[i], h * nj:(h + 1) * nj].reshape(depth, tok) for i in range(lo, hi)], axis=1)

    weight = [w1t, w2b]

    def c_copy(w, i):
        h = chunks[w][i][0]
        part_ = lanes(chunks[w][i])
        return copy(cs.at[w, h, :, part_], cr.at[w, h, :, part_], c_s.at[w, i], c_r.at[w, i], other)

    def project(w, i):
        h, lo, hi = chunks[w][i]
        for place in range(lo, hi):
            arrived(w, h, ORDER[place])
        t = tokens(w, chunks[w][i])
        cs[w, h, :, lo * tok:hi * tok] = dot(weight[w][1 - core], t, 1, 0)
        begin(c_copy(w, i))
        keep[w, h, :, lo * tok:hi * tok] = dot(weight[w][core], t, 1, 0)

    def y_copy(w, i, d):
        h, part_ = chunks[w][i][0], lanes(chunks[w][i])
        return copy(ys.at[w, h, (y + d) % NY, :, part_], yr.at[w, h, d, :, part_],
                    y_s.at[w, i, d - 1], y_r.at[w, i, d - 1], ydev[d])

    def spread(w, i):
        h, lo, hi = chunks[w][i]
        c_copy(w, i).wait_recv()
        total = keep[w, h, :, lo * tok:hi * tok] + cr[w, h, :, lo * tok:hi * tok]
        ys[w, h, :, :, lo * tok:hi * tok] = total.astype(BF16).reshape(NY, rows, (hi - lo) * tok)
        for d in Y_STEPS:
            begin(y_copy(w, i, d))
    along_x(0, 0)
    along_x(0, 1)
    along_x(1, 0)
    along_x(1, 1)
    lw1.wait()
    wcp[0].wait_recv()
    for i in range(2):
        w1t[i] = w1b[i].T
    lw2.wait()
    wcp[1].wait_recv()
    project(0, 0)
    project(0, 1)
    spread(0, 0)
    spread(0, 1)
    project(1, 0)
    spread(1, 0)
    for i in range(1, len(CHUNKS)):
        project(1, i)
    for i in range(1, len(CHUNKS)):
        spread(1, i)

    def a_copy(i, d):
        h, part_ = CHUNKS[i][0], lanes(CHUNKS[i])
        return copy(actf.at[h, core, y, :, part_], actf.at[h, core, y, :, part_],
                    a_s.at[i, d - 1], a_r.at[i, d - 1], ydev[d])

    def act(i):
        h, lo, hi = CHUNKS[i]
        sums = []
        for w in range(2):
            total = ys[w, h, y, :, lo * tok:hi * tok].astype(F32)
            for d in range(1, NY):
                if w == 1:
                    y_copy(w, i, d).wait_recv()
                elif lo == 0:
                    y_copy(w, h, d).wait_recv()
                total = total + yr[w, h, d, :, lo * tok:hi * tok].astype(F32)
            sums.append(total)
        actf[h, core, y, :, lo * tok:hi * tok] = (sums[1] * gelu_slope(sums[0])).astype(BF16)
        for d in Y_STEPS:
            begin(a_copy(i, d))

    def ac_copy(i):
        h, part_ = CHUNKS[i][0], lanes(CHUNKS[i])
        return copy(actf.at[h, core, :, :, part_], actf.at[h, core, :, :, part_], ac_s.at[i], ac_r.at[i], other)

    def to_other(i):
        for d in range(1, NY):
            a_copy(i, d).wait_recv()
        begin(ac_copy(i))

    def hidden_rows(chunk):
        h, lo, hi = chunk
        return actf[h, :, :, :, lo * tok:hi * tok].reshape(NC * NY * rows, (hi - lo) * tok)

    def g_copy(h, r):
        return copy(part.at[r, halves[h]], xin.at[r, halves[h]], gx_s.at[h, r - 1], gx_r.at[h, r - 1], xdev[r])

    own = {}

    def back_to_features(i):
        h, lo, hi = CHUNKS[i]
        ac_copy(i).wait_recv()
        g = hidden_rows(CHUNKS[i])
        half = NY * rows
        value = dot(w1b[0], g[:half], 1, 0) + dot(w1b[1], g[half:], 1, 0)
        for place in range(hi - 1, lo - 1, -1):
            r = ORDER[place]
            this = value[:, (place - lo) * tok:(place - lo + 1) * tok]
            if r == 0:
                own[h] = this
            else:
                part[r, halves[h]] = this.astype(BF16).reshape(nj, feat, tok)
                begin(g_copy(h, r))

    def zz_copy(d):
        return copy(zs.at[(z + d) % nz], zr.at[d], zz_s.at[d - 1], zz_r.at[d - 1], zdev[d])

    def along_z(h, own):
        summed = own.reshape(nj, feat, tok)
        for r in (1, 3, 2):
            g_copy(h, r).wait_recv()
            summed = summed + xin[r, halves[h]].astype(F32)
        zs[halves[h]] = summed.astype(BF16)
        for t in range(h * nj, h * nj + nj):
            d = (t - z + nz) % nz
            unless(t == z, copy(zs.at[t], zr.at[d], zz_s.at[d - 1], zz_r.at[d - 1],
                                (dp, ylo * col + t * NX + x)).start)
    for i in range(len(CHUNKS)):
        act(i)
    to_other(0)
    back_to_features(0)
    for i in range(1, len(CHUNKS)):
        to_other(i)
        back_to_features(i)
    along_z(0, own[0])

    total = sum(dot(tokens(0, c), hidden_rows(c), 1, 1) for c in whole) * scale
    width = wgs.shape[2]
    for i in range(2):
        wgs[i] = total[:, i * width:(i + 1) * width].astype(BF16)
    wcopy = send(wgs.at[1 - ylo], wgr, wg_s.at[0], wg_r.at[0], twin)
    wg_out[half_rows, :] = wgs[ylo]

    along_z(1, own[1])
    result = zs[z].astype(F32)
    for d in range(1, nz):
        zz_copy(d).wait_recv()
        result = result + zr[d].astype(F32)
    fin[...] = result.astype(BF16)

    @pl.when(stays)
    def _():
        ig_out[...] = fin[...]

    @pl.when(jnp.logical_not(stays))
    def _():
        cp = copy(fin, igr, p2_s.at[0], p2_r.at[0], owner(z))
        cp.start()
        cp.wait()
        ig_out[...] = igr[...]

    wcopy.wait_recv()
    wg_out[other_rows, :] = wgr[...]
    for w in range(2):
        for t in range(nz):
            unless(jnp.logical_and(here, z == t), p_copy(w, t).wait_send)
    for d in range(1, nz):
        zz_copy(d).wait_send()
    for cp in pending:
        cp.wait_send()


def body(inputs, out_grad, first_weight, second_weight):
    tok, feat = inputs.shape
    nz = lax.axis_size("mp") // (2 * NX)
    nj = nz // 2
    width = first_weight.shape[1]
    depth = nj * feat
    rows = width // NY
    scale = 1.0 / math.sqrt(tok * lax.axis_size("dp"))
    dma = pltpu.SemaphoreType.DMA
    vmem = pltpu.VMEM
    scratch = [
        vmem((2, NX, nz, feat, tok), BF16),
        vmem((2, feat, tok), BF16),
        vmem((2, depth, width), BF16),
        vmem((2, width, depth), BF16),
        vmem((2, width, depth), BF16),
        vmem((2, 2, width, NX * tok), F32),
        vmem((2, 2, width, NX * tok), F32),
        vmem((2, 2, width, NX * tok), F32),
        vmem((2, 2, NY, rows, NX * tok), BF16),
        vmem((2, 2, NY, rows, NX * tok), BF16),
        vmem((2, NC, NY, rows, NX * tok), BF16),
        vmem((NX, nz, feat, tok), BF16),
        vmem((NX, nz, feat, tok), BF16),
        vmem((nz, feat, tok), BF16),
        vmem((nz, feat, tok), BF16),
        vmem((feat, tok), BF16),
        vmem((feat, tok), BF16),
        vmem((2, depth, width), BF16),
        vmem((depth, width), BF16),
        dma((6,)), dma((2,)), dma((2,)), dma((2, nz)), dma((2, nz)),
        dma((2, 2, 2, NX - 1)), dma((2, 2, 2, NX - 1)), dma((2, 3)), dma((2, 3)),
        dma((2, 3, NY - 1)), dma((2, 3, NY - 1)), dma((3, NY - 1)), dma((3, NY - 1)),
        dma((3,)), dma((3,)), dma((2, NX - 1)), dma((2, NX - 1)), dma((nz - 1,)), dma((nz - 1,)),
        dma((1,)), dma((1,)), dma((1,)), dma((1,)),
    ]
    ig, wg = pl.pallas_call(
        functools.partial(kernel, nz, scale),
        out_shape=(jax.ShapeDtypeStruct((feat, tok), BF16),
                   jax.ShapeDtypeStruct(first_weight.shape, BF16)),
        in_specs=[pl.BlockSpec(memory_space=pl.ANY)] * 4,
        out_specs=(pl.BlockSpec(memory_space=pltpu.VMEM),) * 2,
        scratch_shapes=scratch,
        compiler_params=pltpu.CompilerParams(
            collective_id=0, has_side_effects=True, vmem_limit_bytes=62 * 2 ** 20),
        name="block_backward",
    )(inputs.T, out_grad.T, first_weight, second_weight)
    return (ig.T, wg)


def solution(mesh):
    return jax.shard_map(
        body,
        mesh=mesh,
        in_specs=(P("dp", "mp"), P("dp", "mp"), P("dp", "mp"), P("mp", "dp")),
        out_specs=(P("dp", "mp"), P("dp", "mp")),
        check_vma=False,
    )
```

```python
import functools
import math

import jax
import jax.numpy as jnp
from jax import lax
from jax.experimental import pallas as pl
from jax.experimental.pallas import tpu as pltpu
from jax.sharding import PartitionSpec as P

NX, NY, NC = 4, 8, 2
ORDER = (0, 2, 1, 3)
X_STEPS, Y_STEPS = (2, 1, 3), (4, 3, 5, 2, 6, 1, 7)
CHUNKS = ((0, 0, 4), (1, 0, 4))
F32, BF16 = jnp.float32, jnp.bfloat16
ROOT_HALF, ROOT_TWO_PI = math.sqrt(0.5), math.sqrt(2.0 * math.pi)


def gelu_slope(v):
    cdf = 0.5 * (1.0 + lax.erf(v * ROOT_HALF))
    return cdf + v * jnp.exp(-0.5 * v * v) / ROOT_TWO_PI


def dot(a, b, ca, cb):
    return lax.dot_general(a, b, (((ca,), (cb,)), ((), ())), preferred_element_type=F32)


def kernel(nz, scale, xt, gt, w1, w2, ig_out, wg_out,
           buf, u, w1b, w1t, w2b, cs, cr, keep, ys, yr, actf, part, xin, zs, zr, fin, igr, wgs, wgr,
           loc, w_s, w_r, p_s, p_r, x_s, x_r, c_s, c_r, y_s, y_r, a_s, a_r, ac_s, ac_r,
           gx_s, gx_r, zz_s, zz_r, p2_s, p2_r, wg_s, wg_r):
    nj = nz // 2
    feat, tok = xt.shape
    depth = nj * feat
    col = nz * NX
    rows = ys.shape[3]
    dp, mp = lax.axis_index("dp"), lax.axis_index("mp")
    core, ylo = dp % 2, mp // col
    z, x = (mp % col) // NX, mp % NX
    y = (dp // 2) * 2 + ylo
    pending = []

    def at(x_, y_, z_, c_):
        return ((y_ // 2) * 2 + c_, (y_ % 2) * col + z_ * NX + x_)

    def copy(src, dst, ssem, rsem, dev):
        return pltpu.make_async_remote_copy(
            src_ref=src, dst_ref=dst, send_sem=ssem, recv_sem=rsem,
            device_id=dev, device_id_type=pl.DeviceIdType.MESH)

    def send(*args):
        cp = copy(*args)
        cp.start()
        pending.append(cp)
        return cp

    xdev = [at((x + d) % NX, y, z, core) for d in range(NX)]
    other = at(x, y, z, 1 - core)
    twin = at(x, y + 1 - 2 * ylo, z, core)
    ydev = [at(x, (y + d) % NY, z, core) for d in range(NY)]
    zdev = [at(x, y, (z + d) % nz, core) for d in range(nz)]
    plane = mp // nj
    slot = (dp // NX) * nj + mp % nj
    goals = [(plane // 2, (plane % 2) * col + t * NX + dp % NX) for t in range(nz)]
    here = jnp.logical_and(jnp.logical_and(plane // 2 == dp, plane % 2 == ylo), dp % NX == x)
    stays = jnp.logical_and(here, slot == z)

    def owner(s):
        return ((s // nj) * NX + x, (dp * 2 + ylo) * nj + s % nj)

    def unless(condition, action):
        pl.when(jnp.logical_not(condition))(action)

    half_rows = pl.ds(pl.multiple_of(ylo * depth, 128), depth)
    other_rows = pl.ds(pl.multiple_of((1 - ylo) * depth, 128), depth)
    lu = [pltpu.make_async_copy(xt, u.at[0], loc.at[4]), pltpu.make_async_copy(gt, u.at[1], loc.at[5])]
    for cp in lu:
        cp.start()
    lw1 = pltpu.make_async_copy(w1.at[half_rows, :], w1b.at[ylo], loc.at[0])
    lw2 = pltpu.make_async_copy(w2.at[:, half_rows], w2b.at[ylo], loc.at[1])
    lw1.start()
    lw2.start()

    barrier = pltpu.get_barrier_semaphore()

    def greet(dev):
        pl.semaphore_signal(barrier, inc=1, device_id=dev, device_id_type=pl.DeviceIdType.MESH)

    for s in range(nz):
        unless(jnp.logical_and(here, slot == s), functools.partial(greet, owner(s)))
    unless(stays, lambda: greet((goals[0][0], (plane % 2) * col + slot * NX + dp % NX)))
    for dev in xdev[1:] + [other] + ydev[1:] + zdev[1:]:
        greet(dev)
    peers = (NX - 1) + 1 + (NY - 1) + (nz - 1) + nz + 1
    pl.semaphore_wait(barrier, peers - jnp.where(here, 1, 0) - jnp.where(stays, 1, 0))
    sources = [u.at[0], u.at[1]]
    for cp in lu:
        cp.wait()

    def p_copy(w, t):
        return copy(sources[w], buf.at[w, 0, slot], p_s.at[w, t], p_r.at[w, slot], goals[t])

    def p_local(w):
        return pltpu.make_async_copy(sources[w], buf.at[w, 0, slot], loc.at[2 + w])

    for w in range(2):
        for t in range(nz):
            unless(jnp.logical_and(here, z == t), p_copy(w, t).start)
        pl.when(here)(p_local(w).start)
    wcp = [send(w1.at[other_rows, :], w1b.at[ylo], w_s.at[0], w_r.at[0], twin),
           send(w2.at[:, other_rows], w2b.at[ylo], w_s.at[1], w_r.at[1], twin)]
    for w in range(2):
        pl.when(here)(p_local(w).wait)
    halves = [pl.ds(0, nj), pl.ds(nj, nj)]

    def x_copy(w, h, d):
        return copy(buf.at[w, 0, halves[h]], buf.at[w, NX - d, halves[h]],
                    x_s.at[w, h, d - 1], x_r.at[w, h, d - 1], xdev[d])

    def begin(cp):
        cp.start()
        pending.append(cp)

    def along_x(w, h):
        for s in range(h * nj, h * nj + nj):
            unless(jnp.logical_and(here, slot == s),
                   copy(sources[w], buf.at[w, 0, s], p_s.at[w, 0], p_r.at[w, s], goals[0]).wait_recv)
        for d in X_STEPS:
            begin(x_copy(w, h, d))

    def arrived(w, h, r):
        if r:
            x_copy(w, h, NX - r).wait_recv()

    whole = [(0, 0, NX), (1, 0, NX)]
    chunks = [whole, CHUNKS]

    def lanes(chunk):
        return pl.ds(chunk[1] * tok, (chunk[2] - chunk[1]) * tok)

    def tokens(w, chunk):
        h, lo, hi = chunk
        return jnp.concatenate(
            [buf[w, ORDER[i], h * nj:(h + 1) * nj].reshape(depth, tok) for i in range(lo, hi)], axis=1)

    weight = [w1t, w2b]

    def c_copy(w, i):
        h = chunks[w][i][0]
        part_ = lanes(chunks[w][i])
        return copy(cs.at[w, h, :, part_], cr.at[w, h, :, part_], c_s.at[w, i], c_r.at[w, i], other)

    def project(w, i):
        h, lo, hi = chunks[w][i]
        for place in range(lo, hi):
            arrived(w, h, ORDER[place])
        t = tokens(w, chunks[w][i])
        cs[w, h, :, lo * tok:hi * tok] = dot(weight[w][1 - core], t, 1, 0)
        begin(c_copy(w, i))
        keep[w, h, :, lo * tok:hi * tok] = dot(weight[w][core], t, 1, 0)

    def y_copy(w, i, d):
        h, part_ = chunks[w][i][0], lanes(chunks[w][i])
        return copy(ys.at[w, h, (y + d) % NY, :, part_], yr.at[w, h, d, :, part_],
                    y_s.at[w, i, d - 1], y_r.at[w, i, d - 1], ydev[d])

    def spread(w, i):
        h, lo, hi = chunks[w][i]
        c_copy(w, i).wait_recv()
        total = keep[w, h, :, lo * tok:hi * tok] + cr[w, h, :, lo * tok:hi * tok]
        ys[w, h, :, :, lo * tok:hi * tok] = total.astype(BF16).reshape(NY, rows, (hi - lo) * tok)
        for d in Y_STEPS:
            begin(y_copy(w, i, d))
    along_x(0, 0)
    along_x(0, 1)
    along_x(1, 0)
    along_x(1, 1)
    lw1.wait()
    wcp[0].wait_recv()
    for i in range(2):
        w1t[i] = w1b[i].T
    lw2.wait()
    wcp[1].wait_recv()
    project(0, 0)
    project(0, 1)
    spread(0, 0)
    spread(0, 1)
    project(1, 0)
    spread(1, 0)
    for i in range(1, len(CHUNKS)):
        project(1, i)
    for i in range(1, len(CHUNKS)):
        spread(1, i)

    def a_copy(i, d):
        h, part_ = CHUNKS[i][0], lanes(CHUNKS[i])
        return copy(actf.at[h, core, y, :, part_], actf.at[h, core, y, :, part_],
                    a_s.at[i, d - 1], a_r.at[i, d - 1], ydev[d])

    def act(i):
        h, lo, hi = CHUNKS[i]
        sums = []
        for w in range(2):
            total = ys[w, h, y, :, lo * tok:hi * tok].astype(F32)
            for d in range(1, NY):
                if w == 1:
                    y_copy(w, i, d).wait_recv()
                elif lo == 0:
                    y_copy(w, h, d).wait_recv()
                total = total + yr[w, h, d, :, lo * tok:hi * tok].astype(F32)
            sums.append(total)
        actf[h, core, y, :, lo * tok:hi * tok] = (sums[1] * gelu_slope(sums[0])).astype(BF16)
        for d in Y_STEPS:
            begin(a_copy(i, d))

    def ac_copy(i):
        h, part_ = CHUNKS[i][0], lanes(CHUNKS[i])
        return copy(actf.at[h, core, :, :, part_], actf.at[h, core, :, :, part_], ac_s.at[i], ac_r.at[i], other)

    def to_other(i):
        for d in range(1, NY):
            a_copy(i, d).wait_recv()
        begin(ac_copy(i))

    def hidden_rows(chunk):
        h, lo, hi = chunk
        return actf[h, :, :, :, lo * tok:hi * tok].reshape(NC * NY * rows, (hi - lo) * tok)

    def g_copy(h, r):
        return copy(part.at[r, halves[h]], xin.at[r, halves[h]], gx_s.at[h, r - 1], gx_r.at[h, r - 1], xdev[r])

    own = {}

    def back_to_features(i):
        h, lo, hi = CHUNKS[i]
        ac_copy(i).wait_recv()
        g = hidden_rows(CHUNKS[i])
        half = NY * rows
        value = dot(w1b[0], g[:half], 1, 0) + dot(w1b[1], g[half:], 1, 0)
        for place in range(hi - 1, lo - 1, -1):
            r = ORDER[place]
            this = value[:, (place - lo) * tok:(place - lo + 1) * tok]
            if r == 0:
                own[h] = this
            else:
                part[r, halves[h]] = this.astype(BF16).reshape(nj, feat, tok)
                begin(g_copy(h, r))

    def zz_copy(d):
        return copy(zs.at[(z + d) % nz], zr.at[d], zz_s.at[d - 1], zz_r.at[d - 1], zdev[d])

    def along_z(h, own):
        summed = own.reshape(nj, feat, tok)
        for r in (1, 3, 2):
            g_copy(h, r).wait_recv()
            summed = summed + xin[r, halves[h]].astype(F32)
        zs[halves[h]] = summed.astype(BF16)
        for t in range(h * nj, h * nj + nj):
            d = (t - z + nz) % nz
            unless(t == z, copy(zs.at[t], zr.at[d], zz_s.at[d - 1], zz_r.at[d - 1],
                                (dp, ylo * col + t * NX + x)).start)
    for i in range(len(CHUNKS)):
        act(i)
    to_other(0)
    back_to_features(0)
    for i in range(1, len(CHUNKS)):
        to_other(i)
        back_to_features(i)
    along_z(0, own[0])

    total = sum(dot(tokens(0, c), hidden_rows(c), 1, 1) for c in whole) * scale
    width = wgs.shape[2]
    for i in range(2):
        wgs[i] = total[:, i * width:(i + 1) * width].astype(BF16)
    wcopy = send(wgs.at[1 - ylo], wgr, wg_s.at[0], wg_r.at[0], twin)
    stores = [pltpu.make_async_copy(wgs.at[ylo], wg_out.at[half_rows, :], loc.at[0]),
              pltpu.make_async_copy(wgr, wg_out.at[other_rows, :], loc.at[1])]
    stores[0].start()

    along_z(1, own[1])
    result = zs[z].astype(F32)
    for d in range(1, nz):
        zz_copy(d).wait_recv()
        result = result + zr[d].astype(F32)
    fin[...] = result.astype(BF16)
    home = copy(fin, igr, p2_s.at[0], p2_r.at[0], owner(z))
    unless(stays, home.start)
    wcopy.wait_recv()
    stores[1].start()
    for cp in stores:
        cp.wait()

    @pl.when(stays)
    def _():
        ig_out[...] = fin[...]

    @pl.when(jnp.logical_not(stays))
    def _():
        home.wait()
        ig_out[...] = igr[...]

    for w in range(2):
        for t in range(nz):
            unless(jnp.logical_and(here, z == t), p_copy(w, t).wait_send)
    for d in range(1, nz):
        zz_copy(d).wait_send()
    for cp in pending:
        cp.wait_send()


def body(inputs, out_grad, first_weight, second_weight):
    tok, feat = inputs.shape
    nz = lax.axis_size("mp") // (2 * NX)
    nj = nz // 2
    width = first_weight.shape[1]
    depth = nj * feat
    rows = width // NY
    scale = 1.0 / math.sqrt(tok * lax.axis_size("dp"))
    dma = pltpu.SemaphoreType.DMA
    vmem = pltpu.VMEM
    scratch = [
        vmem((2, NX, nz, feat, tok), BF16),
        vmem((2, feat, tok), BF16),
        vmem((2, depth, width), BF16),
        vmem((2, width, depth), BF16),
        vmem((2, width, depth), BF16),
        vmem((2, 2, width, NX * tok), F32),
        vmem((2, 2, width, NX * tok), F32),
        vmem((2, 2, width, NX * tok), F32),
        vmem((2, 2, NY, rows, NX * tok), BF16),
        vmem((2, 2, NY, rows, NX * tok), BF16),
        vmem((2, NC, NY, rows, NX * tok), BF16),
        vmem((NX, nz, feat, tok), BF16),
        vmem((NX, nz, feat, tok), BF16),
        vmem((nz, feat, tok), BF16),
        vmem((nz, feat, tok), BF16),
        vmem((feat, tok), BF16),
        vmem((feat, tok), BF16),
        vmem((2, depth, width), BF16),
        vmem((depth, width), BF16),
        dma((6,)), dma((2,)), dma((2,)), dma((2, nz)), dma((2, nz)),
        dma((2, 2, NX - 1)), dma((2, 2, NX - 1)), dma((2, 3)), dma((2, 3)),
        dma((2, 3, NY - 1)), dma((2, 3, NY - 1)), dma((3, NY - 1)), dma((3, NY - 1)),
        dma((3,)), dma((3,)), dma((2, NX - 1)), dma((2, NX - 1)), dma((nz - 1,)), dma((nz - 1,)),
        dma((1,)), dma((1,)), dma((1,)), dma((1,)),
    ]
    ig, wg = pl.pallas_call(
        functools.partial(kernel, nz, scale),
        out_shape=(jax.ShapeDtypeStruct((feat, tok), BF16),
                   jax.ShapeDtypeStruct(first_weight.shape, BF16)),
        in_specs=[pl.BlockSpec(memory_space=pl.ANY)] * 4,
        out_specs=(pl.BlockSpec(memory_space=pltpu.VMEM), pl.BlockSpec(memory_space=pl.ANY)),
        scratch_shapes=scratch,
        compiler_params=pltpu.CompilerParams(
            collective_id=0, has_side_effects=True, vmem_limit_bytes=62 * 2 ** 20),
        name="block_backward",
    )(inputs.T, out_grad.T, first_weight, second_weight)
    return (ig.T, wg)


def solution(mesh):
    return jax.shard_map(
        body,
        mesh=mesh,
        in_specs=(P("dp", "mp"), P("dp", "mp"), P("dp", "mp"), P("mp", "dp")),
        out_specs=(P("dp", "mp"), P("dp", "mp")),
        check_vma=False,
    )
```
